32 devices in a mesh: cols: 4 (over y, core), rows: 8 (over z, x).
Axes of the slice: x: 2, y: 2, z: 4, core: 2. Of those that a mesh axis runs over, the one named last changes fastest.
Arguments:
- prior_trials: bfloat16 [256, 64, 1024], P('cols', 'rows'), may hold values from -12 to 12
- courant: bfloat16 [64, 1024], P('rows'), may hold values from 0.039794922 to 0.10986328
- diffusion: bfloat16 [64, 1024], P('rows'), may hold values from 0.1796875 to 0.21972656
- obs_cell: int32 [8, 8, 128], P('rows'), may hold values from 0 to 1023
- obs_count: int32 [8, 8], P('rows', 'cols'), may hold values from 1 to 128, as said below
- obs_value: float32 [8, 8, 128], P('rows', 'cols'), may hold values from -6 to 6
- error_kind: int32 [8, 8, 128], P('rows', 'cols'), may hold values from 0 to 3
- error_std: float32 [4], replicated, may hold values from 0.1 to 0.4
Outputs:
- analysis: bfloat16 [256, 64, 1024], P('cols', 'rows')
The draws below stay inside these ranges and needn't reach their ends.
Inputs may be any that keep to these rules, and one draw needn't show every extreme that they name: `obs_count`: some patch has exactly 128 live slots in every draw.
All inputs are finite; a program needn't handle non-finite values.
Results may differ from the reference program's by a relative error of at most 0.0069.
Values may be sent and summed in bfloat16 or wider, within the bound.
No kernel may reach another device: no remote copies, remote signals or barrier semaphores. Data moves between devices by JAX's collectives and lax.ppermute only.
A program may use at most 64 MiB of HBM per device.

```python
import math
import jax
import jax.numpy as jnp
from jax import lax

TRIAL_COUNT = 256
TILE_NORTH_SPAN = 8
TILE_EAST_SPAN = 128
READING_CAPACITY = 128
FSTEPS = 4
NSIT = 6
NKIND = 4
TILES_NORTHWARD = 8
TILES_EASTWARD = 8
MESH_NORTHWARD = 64
MESH_EASTWARD = 1024


def draw_obs_count(key, part):
    first, second, third = jax.random.split(jax.random.fold_in(key, 11), 3)
    shifts = jax.random.randint(first, (TILES_NORTHWARD, TILES_EASTWARD), 0, 3)
    topmost = jnp.right_shift(jnp.int32(READING_CAPACITY), shifts)
    reduction = jax.random.randint(second, (TILES_NORTHWARD, TILES_EASTWARD), 0, topmost // 2 + 1)
    counts = (topmost - reduction).reshape(-1)
    chosen_spot = jax.random.randint(third, (), 0, TILES_NORTHWARD * TILES_EASTWARD)
    counts = counts.at[chosen_spot].set(READING_CAPACITY)
    return counts.reshape(TILES_NORTHWARD, TILES_EASTWARD).astype(jnp.int32)


def plant(values, own_key, least, top_value):
    shape = values.shape
    place = [jax.random.randint(jax.random.fold_in(own_key, axis), (), 0, shape[axis]) for axis in range(len(shape))]
    values = values.at[tuple(place)].set(least)
    longest = shape.index(max(shape))
    place[longest] = (place[longest] + 1) % shape[longest]
    return values.at[tuple(place)].set(top_value)


def levels(stream_key, dims, cuts, low, top_value):
    def one(axis_at, parts):
        steps = jax.random.uniform(jax.random.fold_in(jax.random.fold_in(stream_key, 6), axis_at), (parts,), jnp.float32, low / len(cuts), top_value / len(cuts))
        return jnp.repeat(jnp.exp(steps), dims[axis_at] // parts).reshape((-1,) + (1,) * (len(dims) - axis_at - 1))

    level = one(*cuts[0])
    for cut in cuts[1:]:
        level = level * one(*cut)
    return level


def gaussian(own_key, shape, deviation, limit, shards=(), kind=jnp.bfloat16):
    gain = levels(own_key, shape, shards, -0.22, 0.18) if shards else 1.0
    entries = jax.random.normal(own_key, shape, jnp.float32) * deviation * gain
    return jnp.minimum(jnp.maximum(entries, -limit), limit).astype(kind)


def setup_inputs(seed: int = 0) -> dict:
    streams_of = jax.random.split(jax.random.key(seed), 9)
    prior_trials = gaussian(streams_of[0], (TRIAL_COUNT, MESH_NORTHWARD, MESH_EASTWARD), 2.0, 12.0, ((0, 4), (1, 8)))
    courant = jnp.clip(0.039794922 + 0.07006836 * jax.random.uniform(streams_of[1], (MESH_NORTHWARD, MESH_EASTWARD), jnp.float32) ** levels(streams_of[1], (MESH_NORTHWARD, MESH_EASTWARD), ((0, 8),), -0.2, 0.2), 0.039794922, 0.10986328).astype(jnp.bfloat16)
    diffusion = jnp.clip(0.1796875 + 0.040039062 * jax.random.uniform(streams_of[2], (MESH_NORTHWARD, MESH_EASTWARD), jnp.float32) ** levels(streams_of[2], (MESH_NORTHWARD, MESH_EASTWARD), ((0, 8),), -0.2, 0.2), 0.1796875, 0.21972656).astype(jnp.bfloat16)
    obs_cell = plant(jax.random.randint(streams_of[3], (TILES_NORTHWARD, TILES_EASTWARD, READING_CAPACITY), 0, TILE_NORTH_SPAN * TILE_EAST_SPAN), jax.random.fold_in(streams_of[3], 1), 0, (TILE_NORTH_SPAN * TILE_EAST_SPAN) - 1).astype(jnp.int32)
    obs_count = draw_obs_count(jax.random.fold_in(streams_of[8], 71), 0)
    obs_value = gaussian(streams_of[5], (TILES_NORTHWARD, TILES_EASTWARD, READING_CAPACITY), 1.0, 6.0, ((0, 8), (1, 4)), jnp.float32)
    error_kind = plant(jax.random.randint(streams_of[6], (TILES_NORTHWARD, TILES_EASTWARD, READING_CAPACITY), 0, NKIND), jax.random.fold_in(streams_of[6], 1), 0, NKIND - 1).astype(jnp.int32)
    error_std = jnp.clip(jnp.exp(jax.random.uniform(streams_of[7], (NKIND,), jnp.float32, math.log(0.1), math.log(0.4))), 0.1, 0.4)
    return {"prior_trials": prior_trials, "courant": courant, "diffusion": diffusion, "obs_cell": obs_cell, "obs_count": obs_count, "obs_value": obs_value, "error_kind": error_kind, "error_std": error_std}


highest = lax.Precision.HIGHEST

def advance(member_index, speed_field, spread_field):
    for iteration in range(FSTEPS):
        padded = jnp.pad(member_index, 1)
        upwind = padded[:-2, 1:-1]
        downwind = padded[2:, 1:-1]
        west_side = padded[1:-1, :-2]
        east_side = padded[1:-1, 2:]
        member_index = member_index - speed_field * (member_index - upwind) + spread_field * (upwind + downwind + west_side + east_side - 4.0 * member_index)
    return member_index

def transform(obs_block, center_y, center_x):
    members = obs_block.shape[0] - 4
    values = obs_block[:members]
    observed = obs_block[members]
    inverse = obs_block[members + 1]
    coord_y = obs_block[members + 2]
    coord_x = obs_block[members + 3]
    average = lax.optimization_barrier(jnp.mean(values, axis=0))
    spread_obs = values - average
    localized = inverse * jnp.exp(-0.5 * ((coord_y - center_y) / TILE_NORTH_SPAN) ** 2 - 0.5 * ((coord_x - center_x) / TILE_EAST_SPAN) ** 2)
    weighted = spread_obs * localized
    factor = float(members - 1)
    identity = jnp.eye(members, dtype=values.dtype)
    system = identity + jnp.dot(weighted, spread_obs.T, precision=highest) / factor
    frobenius = jnp.sqrt(jnp.sum(system * system))
    iterate = system / frobenius
    inverse_root = identity
    for iteration in range(NSIT):
        middle = 1.5 * identity - 0.5 * jnp.dot(inverse_root, iterate, precision=highest)
        iterate = jnp.dot(iterate, middle, precision=highest)
        inverse_root = jnp.dot(middle, inverse_root, precision=highest)
    weights_root = inverse_root / jnp.sqrt(frobenius)
    inverse_full = jnp.dot(weights_root, weights_root, precision=highest)
    mean_gain = jnp.dot(inverse_full, jnp.dot(weighted, observed - average, precision=highest), precision=highest) / factor
    combined = weights_root + mean_gain[:, None]
    mixing = combined - lax.optimization_barrier(jnp.mean(combined, axis=0, keepdims=True)) + 1.0 / members
    return mixing.astype(jnp.bfloat16)

def reference(prior_trials, courant, diffusion, obs_cell, obs_count, obs_value, error_kind, error_std):
    speed_field = courant.astype(jnp.float32)
    spread_field = diffusion.astype(jnp.float32)

    def advanced_trial(member_index):
        return advance(member_index.astype(jnp.float32), speed_field, spread_field).astype(jnp.bfloat16)
    propagated_surface = lax.map(advanced_trial, prior_trials)
    patch_row = jnp.arange(TILES_NORTHWARD, dtype=jnp.int32)[:, None, None]
    patch_col = jnp.arange(TILES_EASTWARD, dtype=jnp.int32)[None, :, None]
    cell_y = patch_row * TILE_NORTH_SPAN + obs_cell // TILE_EAST_SPAN
    cell_x = patch_col * TILE_EAST_SPAN + obs_cell % TILE_EAST_SPAN
    flattened_position = (cell_y * MESH_EASTWARD + cell_x).reshape(-1)
    drawn_readings = jnp.take(propagated_surface.reshape(TRIAL_COUNT, MESH_NORTHWARD * MESH_EASTWARD), flattened_position, axis=1).astype(jnp.float32).reshape(TRIAL_COUNT, TILES_NORTHWARD, TILES_EASTWARD, READING_CAPACITY)
    live_mask = jnp.arange(READING_CAPACITY, dtype=jnp.int32)[None, None, :] < obs_count[:, :, None]
    chosen = error_std[error_kind]
    inverse = jnp.where(live_mask, 1.0 / (chosen * chosen), jnp.zeros_like(chosen))
    obs_block = jnp.concatenate([drawn_readings, obs_value[None], inverse[None], cell_y.astype(jnp.float32)[None], cell_x.astype(jnp.float32)[None]], axis=0)
    padded = jnp.pad(obs_block, ((0, 0), (1, 1), (1, 1), (0, 0)))

    def one_patch(patch_number):
        tile_start_northward = patch_number // TILES_EASTWARD
        tile_start_eastward = patch_number % TILES_EASTWARD
        beside_all = lax.dynamic_slice(padded, (jnp.int32(0), tile_start_northward, tile_start_eastward, jnp.int32(0)), (TRIAL_COUNT + 4, 3, 3, READING_CAPACITY)).reshape(TRIAL_COUNT + 4, 9 * READING_CAPACITY)
        center_y = tile_start_northward.astype(jnp.float32) * TILE_NORTH_SPAN + (TILE_NORTH_SPAN - 1) / 2.0
        center_x = tile_start_eastward.astype(jnp.float32) * TILE_EAST_SPAN + (TILE_EAST_SPAN - 1) / 2.0
        mixing = transform(beside_all, center_y, center_x)
        tile_point_count = lax.dynamic_slice(propagated_surface, (jnp.int32(0), tile_start_northward * TILE_NORTH_SPAN, tile_start_eastward * TILE_EAST_SPAN), (TRIAL_COUNT, TILE_NORTH_SPAN, TILE_EAST_SPAN))
        return jnp.einsum('jyx,jk->kyx', tile_point_count.astype(jnp.float32), mixing.astype(jnp.float32)).astype(jnp.bfloat16)
    pieces = lax.map(one_patch, jnp.arange(TILES_NORTHWARD * TILES_EASTWARD, dtype=jnp.int32))
    return pieces.reshape(TILES_NORTHWARD, TILES_EASTWARD, TRIAL_COUNT, TILE_NORTH_SPAN, TILE_EAST_SPAN).transpose(2, 0, 3, 1, 4).reshape(TRIAL_COUNT, MESH_NORTHWARD, MESH_EASTWARD)
```

```python
import functools
import jax
import jax.numpy as jnp
from jax import lax
from jax.experimental import pallas as pl
from jax.experimental.pallas import tpu as pltpu
from jax.sharding import PartitionSpec as P

ROWS = 8
LANES = 128
FSTEPS = 4
NSIT = 6
BLOCK = 16
LIMIT = 56 * 1024 * 1024
f32 = jnp.float32
bf16 = jnp.bfloat16

vmem = functools.partial(pl.BlockSpec, memory_space=pltpu.VMEM)
smem = functools.partial(pl.BlockSpec, memory_space=pltpu.SMEM)


def call(kernel, outs, scratch, flops, moved, args, specs):
    return pl.pallas_call(
        kernel,
        out_shape=outs,
        in_specs=specs,
        out_specs=[vmem() for _ in outs],
        scratch_shapes=scratch,
        compiler_params=pltpu.CompilerParams(vmem_limit_bytes=LIMIT),
        cost_estimate=pl.CostEstimate(flops=flops, bytes_accessed=moved, transcendentals=0),
    )(*args)


def forecast_kernel(first, offset, m, groups, me_ref, own_ref, up_ref, down_ref, *rest):
    if first:
        speed_ref, spread_ref, cell_ref = rest[:3]
        rest = rest[3:]
        coef_ref, sample_ref = rest[:2]
        rest = rest[2:]
    else:
        coef_ref, cell_ref, sample_ref = rest[:3]
        rest = rest[3:]
    parts = rest[:groups]
    even, odd = rest[groups:]
    width = own_ref.shape[2]
    tiles = width // LANES
    span = width // groups
    total = ROWS + 2 * FSTEPS
    if first:
        base = FSTEPS * m
        up_c = up_ref[base : base + BLOCK, :].astype(f32)
        down_c = down_ref[base : base + BLOCK, :].astype(f32)
        speed = jnp.concatenate(
            [up_c[:FSTEPS], speed_ref[...].astype(f32), down_c[:FSTEPS]], axis=0
        )
        spread = jnp.concatenate(
            [up_c[FSTEPS : 2 * FSTEPS], spread_ref[...].astype(f32), down_c[FSTEPS : 2 * FSTEPS]],
            axis=0,
        )
        coef_ref[0] = 1.0 - speed - 4.0 * spread
        coef_ref[1] = speed + spread
        coef_ref[2] = spread
    me = me_ref[0]
    lane = lax.broadcasted_iota(jnp.int32, (8, LANES), 1)
    leftmost = lane == 0
    rightmost = lane == LANES - 1

    def block(i, carry):
        start = pl.multiple_of(i * BLOCK, BLOCK)
        for r in range(FSTEPS):
            at = pl.multiple_of(r * m + start, BLOCK)
            even[r] = up_ref[pl.ds(at, BLOCK), :].astype(f32)
            even[r + FSTEPS + ROWS] = down_ref[pl.ds(at, BLOCK), :].astype(f32)
        for r in range(ROWS):
            even[r + FSTEPS] = own_ref[
                r, pl.ds(pl.multiple_of(offset + start, BLOCK), BLOCK), :
            ].astype(f32)
        source, target = even, odd
        for step in range(1, FSTEPS + 1):
            for half in range(0, BLOCK, 8):

                def row(r):
                    return [
                        source[r, half : half + 8, t * LANES : (t + 1) * LANES]
                        for t in range(tiles)
                    ]

                above, centre = row(step - 1), row(step)
                for r in range(step, total - step):
                    below = row(r + 1)
                    right = [pltpu.roll(c, 1, 1) for c in centre]
                    left = [pltpu.roll(c, LANES - 1, 1) for c in centre]
                    for t in range(tiles):
                        cut = slice(t * LANES, (t + 1) * LANES)
                        west = jnp.where(leftmost, right[t - 1] if t else 0.0, right[t])
                        east = jnp.where(
                            rightmost, left[t + 1] if t + 1 < tiles else 0.0, left[t]
                        )
                        target[r, half : half + 8, cut] = (
                            coef_ref[0, r : r + 1, cut] * centre[t]
                            + coef_ref[1, r : r + 1, cut] * above[t]
                            + coef_ref[2, r : r + 1, cut] * (below[t] + (west + east))
                        )
                    above, centre = centre, below
            source, target = target, source
        for t in range(tiles):
            cell = cell_ref[t : t + 1, :]
            at_row = jnp.broadcast_to(cell // LANES, (8, LANES))
            at_lane = jnp.broadcast_to(cell % LANES, (8, LANES))
            halves = []
            for half in range(0, BLOCK, 8):
                taken = jnp.zeros((8, LANES), f32)
                for y in range(ROWS):
                    values = source[
                        y + FSTEPS, half : half + 8, t * LANES : (t + 1) * LANES
                    ]
                    picked = jnp.take_along_axis(
                        values, at_lane, axis=1, mode="promise_in_bounds"
                    )
                    taken = jnp.where(at_row == y, picked, taken)
                halves.append(taken)
            sample_ref[pl.ds(start, BLOCK), t * LANES : (t + 1) * LANES] = jnp.concatenate(
                halves, axis=0
            ).astype(bf16)
        for d in range(groups):
            column = pl.multiple_of((me ^ d) * span, LANES)
            for y in range(ROWS):
                parts[d][y, pl.ds(start, BLOCK), :] = source[
                    y + FSTEPS, :, pl.ds(column, span)
                ].astype(bf16)
        return carry

    lax.fori_loop(0, m // BLOCK, block, 0)


def forecast(first, offset, m, groups, me, own, up, down, extra, cell):
    width = own.shape[2]
    total = ROWS + 2 * FSTEPS
    outs = []
    if first:
        outs.append(jax.ShapeDtypeStruct((3, total, width), f32))
    outs.append(jax.ShapeDtypeStruct((m, width), bf16))
    outs += [jax.ShapeDtypeStruct((ROWS, m, width // groups), bf16) for _ in range(groups)]
    args = (me, own, up, down) + tuple(extra) + (cell,)
    scratch = [pltpu.VMEM((total, BLOCK, width), f32)] * 2
    return call(
        functools.partial(forecast_kernel, first, offset, m, groups),
        outs,
        scratch,
        44 * m * width * 16,
        m * width * 2 * 30,
        args,
        [smem()] + [vmem()] * (len(args) - 1),
    )


def spread_kernel(groups, m, me_ref, up_ref, own_ref, down_ref, *rest):
    parts, padded = rest[:groups], rest[groups]
    width = own_ref.shape[1]
    span = width // groups
    me = me_ref[0]
    blank = jnp.zeros((m, LANES), bf16)
    for i, ref in enumerate((up_ref, own_ref, down_ref)):
        padded[i, :, :LANES] = blank
        padded[i, :, LANES + width :] = blank
        padded[i, :, LANES : LANES + width] = ref[...]
    for d in range(groups):
        column = pl.multiple_of((me ^ d) * span, LANES)
        for i in range(3):
            parts[d][i] = padded[i, :, pl.ds(column, span + 2 * LANES)]


def spread_samples(groups, me, up, own, down):
    m, width = own.shape
    wide = width // groups + 2 * LANES
    return call(
        functools.partial(spread_kernel, groups, m),
        [jax.ShapeDtypeStruct((3, m, wide), bf16) for _ in range(groups)],
        [pltpu.VMEM((3, m, width + 2 * LANES), bf16)],
        0,
        m * width * 12,
        (me, up, own, down),
        [smem()] + [vmem()] * 3,
    )


def product(a, b):
    return jnp.dot(a, b, preferred_element_type=f32)


def halves_of(a):
    high = a.astype(bf16)
    return high, (a - high.astype(f32)).astype(bf16)


def wide_product(a, b):
    return product(a[0], b[0]) + (product(a[0], b[1]) + product(a[1], b[0]))


def transform_kernel(groups, chunks, left_ref, mid_ref, right_ref, *rest):
    count = groups * len(chunks)
    sample_refs = rest[:count]
    field_refs = rest[count : 2 * count]
    outs = rest[2 * count : 2 * count + groups]
    values, turned = rest[2 * count + groups :]
    tile_trials = sum(chunks)
    members = groups * tile_trials
    patches = mid_ref.shape[1] // LANES
    wide = patches + 2
    for d in range(groups):
        at = d * tile_trials
        for j, m in enumerate(chunks):
            ref = sample_refs[j * groups + d]
            for i in range(3):
                values[i, at : at + m, :] = ref[i]
            at += m
    meta = jnp.concatenate([left_ref[...], mid_ref[...], right_ref[...]], axis=1)
    deviation = [[None] * wide for _ in range(3)]
    gap = [[None] * wide for _ in range(3)]
    for i in range(3):
        for t in range(wide):
            cut = slice(t * LANES, (t + 1) * LANES)
            entry = values[i, :, cut].astype(f32)
            average = jnp.sum(entry, axis=0, keepdims=True) * (1.0 / members)
            deviation[i][t] = entry - average
            gap[i][t] = meta[8 * i : 8 * i + 1, cut] - average
    factor = float(members - 1)
    row_id = lax.broadcasted_iota(jnp.int32, (members, members), 0)
    col_id = lax.broadcasted_iota(jnp.int32, (members, members), 1)
    diagonal = row_id == col_id
    state = []
    for q in range(patches):
        pieces = []
        pull = jnp.zeros((members, LANES), f32)
        for i in range(3):
            for t in range(q, q + 3):
                cut = slice(t * LANES, (t + 1) * LANES)
                inverse = meta[8 * i + 1 : 8 * i + 2, cut]
                cell_y = meta[8 * i + 2 : 8 * i + 3, cut]
                cell_x = meta[8 * i + 3 : 8 * i + 4, cut]
                off_y = ((i - 1) * ROWS + cell_y - (ROWS - 1) / 2.0) / ROWS
                off_x = ((t - q - 1) * LANES + cell_x - (LANES - 1) / 2.0) / LANES
                local = inverse * jnp.exp(-0.5 * off_y * off_y - 0.5 * off_x * off_x)
                weight = jnp.sqrt(local * (1.0 / factor))
                pieces.append((deviation[i][t] * weight).astype(bf16))
                pull = pull + deviation[i][t] * (local * (1.0 / factor) * gap[i][t])
        scaled = jnp.concatenate(pieces, axis=1)
        gram = lax.dot_general(
            scaled, scaled, (((1,), (1,)), ((), ())), preferred_element_type=f32
        )
        system = jnp.where(diagonal, gram + 1.0, gram)
        squared = jnp.sum(system * system, axis=0, keepdims=True)
        squared = jnp.sum(squared, axis=1, keepdims=True)
        scale = jnp.sqrt(squared)
        state.append([system * (1.0 / scale), None, scale, jnp.sum(pull, axis=1, keepdims=True)])
    for step in range(NSIT):
        fine = step >= NSIT - 2
        for s in state:
            w, z = s[0], s[1]
            if fine:
                half = halves_of(w * -0.5)
                mul = lambda a: wide_product(halves_of(a), half)
            else:
                half = (w * -0.5).astype(bf16)
                mul = lambda a: product(a.astype(bf16), half)
            if z is None:
                s[1] = jnp.where(diagonal, 1.5, 0.0) - 0.5 * w
            else:
                s[1] = 1.5 * z + mul(z)
            if step < NSIT - 1:
                between = 1.5 * w + mul(w)
                s[0] = 1.5 * between + mul(between)
    for q in range(patches):
        _, z, scale, pull = state[q]
        root = z * lax.rsqrt(scale)
        once = jnp.sum(root * pull, axis=0, keepdims=True)
        gain = jnp.sum(root * once, axis=1, keepdims=True)
        middle = jnp.sum(root, axis=0, keepdims=True) * (1.0 / members)
        shift = gain - jnp.sum(gain, axis=0, keepdims=True) * (1.0 / members) + 1.0 / members
        mixing = ((root - middle) + shift).astype(bf16)
        pieces = []
        for y in range(ROWS):
            column = []
            for d in range(groups):
                for j in range(len(chunks)):
                    column.append(
                        field_refs[j * groups + d][y, :, q * LANES : (q + 1) * LANES]
                    )
            pieces.append(jnp.concatenate(column, axis=0))
        field = jnp.concatenate(pieces, axis=1)
        result = lax.dot_general(
            mixing, field, (((0,), (0,)), ((), ())), preferred_element_type=f32
        )
        for y in range(ROWS):
            turned[pl.ds(y, members, stride=ROWS), :] = result[:, y * LANES : (y + 1) * LANES]
        for d in range(groups):
            at = d * tile_trials * ROWS
            outs[d][:, :, q * LANES : (q + 1) * LANES] = (
                turned[at : at + tile_trials * ROWS, :]
                .reshape(tile_trials, ROWS, LANES)
                .astype(bf16)
            )


def transform(groups, chunks, meta, samples, fields):
    span = meta[1].shape[1]
    tile_trials = sum(chunks)
    members = groups * tile_trials
    args = tuple(meta) + tuple(samples) + tuple(fields)
    return call(
        functools.partial(transform_kernel, groups, chunks),
        [jax.ShapeDtypeStruct((tile_trials, ROWS, span), bf16) for _ in range(groups)],
        [
            pltpu.VMEM((3, members, span + 2 * LANES), bf16),
            pltpu.VMEM((members * ROWS, LANES), f32),
        ],
        4 * 10**9,
        4 * 2**20,
        args,
        [vmem()] * len(args),
    )


def gather_kernel(groups, me_ref, *rest):
    parts, out_ref = rest[:groups], rest[groups]
    span = parts[0].shape[2]
    me = me_ref[0]
    for d in range(groups):
        column = pl.multiple_of((me ^ d) * span, LANES)
        out_ref[:, :, pl.ds(column, span)] = parts[d][...]


def gathered(groups, me, parts):
    tile_trials, rows, span = parts[0].shape
    return call(
        functools.partial(gather_kernel, groups),
        [jax.ShapeDtypeStruct((tile_trials, rows, span * groups), bf16)],
        [],
        0,
        4 * tile_trials * rows * span * groups,
        (me,) + tuple(parts),
        [smem()] + [vmem()] * groups,
    )[0]


def across(parts):
    groups = len(parts)
    out = list(parts)
    for d in sorted(range(1, groups), reverse=True):
        out[d] = lax.ppermute(parts[d], "cols", [(i, i ^ d) for i in range(groups)])
    return out


def up_down(to_next, to_before, axis):
    count = lax.axis_size(axis)
    forward = [(i, i + 1) for i in range(count - 1)]
    back = [(j, i) for i, j in forward]
    return lax.ppermute(to_next, axis, forward), lax.ppermute(to_before, axis, back)


def on_device(
    prior_trials, courant, diffusion, obs_cell, obs_count, obs_value, error_kind, error_std
):
    tile_trials, _, width = prior_trials.shape
    groups = lax.axis_size("cols")
    own_count = obs_count.shape[1]
    slots = obs_cell.shape[2]
    me_scalar = lax.axis_index("cols").astype(jnp.int32)
    me = me_scalar[None]
    chunks = (tile_trials - BLOCK, BLOCK) if tile_trials > BLOCK else (tile_trials,)

    turned = jnp.transpose(prior_trials, (1, 0, 2))
    blank = jnp.zeros((BLOCK - 2 * FSTEPS, width), bf16)
    halos = []
    offset = 0
    for j, m in enumerate(chunks):
        pair = []
        for low in (ROWS - FSTEPS, 0):
            message = turned[low : low + FSTEPS, offset : offset + m].reshape(FSTEPS * m, width)
            if j == 0:
                message = jnp.concatenate(
                    [
                        message,
                        courant[low : low + FSTEPS],
                        diffusion[low : low + FSTEPS],
                        blank,
                    ],
                    axis=0,
                )
            pair.append(message)
        halos.append(up_down(pair[0], pair[1], "rows"))
        offset += m

    own_cell = lax.dynamic_slice_in_dim(obs_cell, me_scalar * own_count, own_count, 1)[0]
    live = jnp.arange(slots, dtype=jnp.int32)[None, :] < obs_count[0][:, None]
    table = 1.0 / (error_std * error_std)
    kinds = jnp.arange(error_std.shape[0], dtype=jnp.int32)
    looked = jnp.sum(jnp.where(error_kind[0][:, :, None] == kinds, table, 0.0), axis=-1)
    inverse = jnp.where(live, looked, 0.0)
    known = jnp.stack(
        [
            obs_value[0].reshape(-1),
            inverse.reshape(-1),
            (own_cell // LANES).astype(f32).reshape(-1),
            (own_cell % LANES).astype(f32).reshape(-1),
        ],
        axis=0,
    )
    known = jnp.pad(known, ((0, 4), (0, 0)))
    above, below = up_down(known, known, "rows")
    middle = jnp.concatenate([above, known, below], axis=0)
    left, right = up_down(middle[:, -LANES:], middle[:, :LANES], "cols")

    coef = None
    offset = 0
    samples, fields = [], []
    for j, m in enumerate(chunks):
        up, down = halos[j]
        extra = (courant, diffusion) if j == 0 else (coef,)
        made = forecast(j == 0, offset, m, groups, me, turned, up, down, extra, obs_cell[0])
        if j == 0:
            coef, made = made[0], made[1:]
        sampled, parts = made[0], made[1:]
        from_up, from_down = up_down(sampled, sampled, "rows")
        fields += across(parts)
        samples += across(spread_samples(groups, me, from_up, sampled, from_down))
        offset += m
    analysis = transform(groups, chunks, (left, middle, right), samples, fields)
    return gathered(groups, me, across(analysis))


def solution(mesh):
    placed = (
        P("cols", "rows", None),
        P("rows", None),
        P("rows", None),
        P("rows", None, None),
        P("rows", "cols"),
        P("rows", "cols", None),
        P("rows", "cols", None),
        P(),
    )
    return jax.shard_map(
        on_device, mesh=mesh, in_specs=placed, out_specs=P("cols", "rows", None), check_vma=False
    )
```

```python
import functools
import math
import jax
import jax.numpy as jnp
from jax import lax
from jax.experimental import pallas as pl
from jax.experimental.pallas import tpu as pltpu
from jax.sharding import PartitionSpec as P

ROWS = 8
LANES = 128
FSTEPS = 4
NSIT = 6
BLOCK = 16
SLACK = 12 * 1024 * 1024
f32 = jnp.float32
bf16 = jnp.bfloat16

vmem = functools.partial(pl.BlockSpec, memory_space=pltpu.VMEM)
smem = functools.partial(pl.BlockSpec, memory_space=pltpu.SMEM)


def call(kernel, outs, scratch, flops, args, specs):
    moved = sum(x.size * x.dtype.itemsize for x in tuple(args) + tuple(outs))
    held = sum(math.prod(x.shape) * jnp.dtype(x.dtype).itemsize for x in scratch)
    return pl.pallas_call(
        kernel,
        out_shape=outs,
        in_specs=specs,
        out_specs=[vmem() for _ in outs],
        scratch_shapes=scratch,
        compiler_params=pltpu.CompilerParams(vmem_limit_bytes=moved + held + SLACK),
        cost_estimate=pl.CostEstimate(flops=flops, bytes_accessed=moved, transcendentals=0),
    )(*args)


def pack_kernel(chunks, place_ref, prior_ref, speed_ref, spread_ref, *rest):
    messages, flat = rest[:-1], rest[-1]
    odd = place_ref[1]

    def fill(first_low, second_low):
        offset = 0
        for j, m in enumerate(chunks):
            pair = messages[2 * j : 2 * j + 2]

            def block(i, carry):
                start = pl.multiple_of(i * BLOCK, BLOCK)
                for t in range(flat.shape[0]):
                    cut = slice(t * LANES, (t + 1) * LANES)
                    entry = prior_ref[pl.ds(offset + start, BLOCK), :, cut].astype(f32)
                    flat[t] = entry.reshape(BLOCK * ROWS, LANES)
                    for ref, low in zip(pair, (first_low, second_low)):
                        for r in range(FSTEPS):
                            at = pl.multiple_of(r * m + start, BLOCK)
                            ref[pl.ds(at, BLOCK), cut] = flat[
                                t, pl.ds(low + r, BLOCK, stride=ROWS), :
                            ].astype(bf16)
                return carry

            lax.fori_loop(0, m // BLOCK, block, 0)
            if j == 0:
                speed = speed_ref[...].astype(f32)
                spread = spread_ref[...].astype(f32)
                blank = jnp.zeros((BLOCK - 2 * FSTEPS, speed.shape[1]), f32)
                for ref, low in zip(pair, (first_low, second_low)):
                    ref[FSTEPS * m :, :] = jnp.concatenate(
                        [speed[low : low + FSTEPS], spread[low : low + FSTEPS], blank], axis=0
                    ).astype(bf16)
            offset += m

    pl.when(odd == 1)(lambda: fill(0, FSTEPS))
    pl.when(odd == 0)(lambda: fill(FSTEPS, 0))


def packed(chunks, place, prior, speed, spread):
    width = prior.shape[2]
    outs = []
    for j, m in enumerate(chunks):
        rows = FSTEPS * m + (BLOCK if j == 0 else 0)
        outs += [jax.ShapeDtypeStruct((rows, width), bf16)] * 2
    return call(
        functools.partial(pack_kernel, chunks),
        outs,
        [pltpu.VMEM((width // LANES, BLOCK * ROWS, LANES), f32)],
        0,
        (place, prior, speed, spread),
        [smem()] + [vmem()] * 3,
    )


def thirds_of(x):
    high = x.astype(bf16).astype(f32)
    middle = (x - high).astype(bf16).astype(f32)
    return [high, middle, (x - high) - middle]


def describe(m, me, sample_ref, cell_ref, value_ref, kind_ref, count_ref, std_ref):
    sample_ref[m : m + BLOCK, :] = jnp.zeros((BLOCK, sample_ref.shape[1]), bf16)
    own_count, slots = value_ref.shape[1:]
    slot = lax.broadcasted_iota(jnp.int32, (1, slots), 1)
    blank = jnp.zeros((BLOCK - 8, slots), f32)
    for q in range(own_count):
        patch = me * own_count + q
        cell = cell_ref[pl.ds(patch, 1), :]
        kind = kind_ref[0, q : q + 1, :]
        inverse = jnp.zeros((1, slots), f32)
        for k in range(std_ref.shape[0]):
            deviation = jnp.full((1, slots), std_ref[k], f32)
            inverse = jnp.where(kind == k, 1.0 / (deviation * deviation), inverse)
        inverse = jnp.where(slot < count_ref[0, q], inverse, 0.0)
        terms = thirds_of(value_ref[0, q : q + 1, :]) + thirds_of(inverse)
        terms += [(cell // LANES).astype(f32), (cell % LANES).astype(f32), blank]
        column = pl.multiple_of(patch * LANES, LANES)
        sample_ref[m : m + BLOCK, pl.ds(column, LANES)] = jnp.concatenate(
            terms, axis=0
        ).astype(bf16)


def forecast_kernel(
    first, m, place_ref, near_ref, far_ref, from_near_ref, from_far_ref, cell_ref, *rest
):
    if first:
        value_ref, kind_ref, count_ref, std_ref, coef_ref, sample_ref = rest[:6]
        rest = rest[6:]
        before = 0
    else:
        coef_ref, earlier_ref, sample_ref = rest[:3]
        rest = rest[3:]
        before = earlier_ref.shape[0] - BLOCK
        sample_ref[:before, :] = earlier_ref[:before, :]
        sample_ref[before + m :, :] = earlier_ref[before:, :]
    field_ref, even, odd = rest
    width = near_ref.shape[1]
    tiles = width // LANES
    total = ROWS + 2 * FSTEPS
    me, is_odd = place_ref[0], place_ref[1]
    sources = (
        (from_near_ref, (1 - is_odd) * (FSTEPS + ROWS)),
        (near_ref, FSTEPS + (1 - is_odd) * FSTEPS),
        (far_ref, FSTEPS + is_odd * FSTEPS),
        (from_far_ref, is_odd * (FSTEPS + ROWS)),
    )
    if first:
        base = FSTEPS * m
        tails = [ref[base : base + BLOCK, :].astype(f32) for ref, _ in sources]
        tails = [jnp.where(is_odd == 1, tails[k], tails[3 - k]) for k in range(4)]
        speed = jnp.concatenate([x[:FSTEPS] for x in tails], axis=0)
        spread = jnp.concatenate([x[FSTEPS : 2 * FSTEPS] for x in tails], axis=0)
        coef_ref[0] = 1.0 - speed - 4.0 * spread
        coef_ref[1] = speed + spread
        coef_ref[2] = spread
        describe(m, me, sample_ref, cell_ref, value_ref, kind_ref, count_ref, std_ref)
    lane = lax.broadcasted_iota(jnp.int32, (8, LANES), 1)
    leftmost = lane == 0
    rightmost = lane == LANES - 1

    def block(i, carry):
        start = pl.multiple_of(i * BLOCK, BLOCK)
        for ref, first_row in sources:
            for r in range(FSTEPS):
                at = pl.multiple_of(r * m + start, BLOCK)
                even[first_row + r] = ref[pl.ds(at, BLOCK), :].astype(f32)
        source, target = even, odd
        for step in range(1, FSTEPS + 1):
            for half in range(0, BLOCK, 8):

                def row(r):
                    return [
                        source[r, half : half + 8, t * LANES : (t + 1) * LANES]
                        for t in range(tiles)
                    ]

                above, centre = row(step - 1), row(step)
                for r in range(step, total - step):
                    below = row(r + 1)
                    right = [pltpu.roll(c, 1, 1) for c in centre]
                    left = [pltpu.roll(c, LANES - 1, 1) for c in centre]
                    for t in range(tiles):
                        cut = slice(t * LANES, (t + 1) * LANES)
                        west = jnp.where(leftmost, right[t - 1] if t else 0.0, right[t])
                        east = jnp.where(
                            rightmost, left[t + 1] if t + 1 < tiles else 0.0, left[t]
                        )
                        target[r, half : half + 8, cut] = (
                            coef_ref[0, r : r + 1, cut] * centre[t]
                            + coef_ref[1, r : r + 1, cut] * above[t]
                            + coef_ref[2, r : r + 1, cut] * (below[t] + (west + east))
                        )
                    above, centre = centre, below
            source, target = target, source
        for t in range(tiles):
            cell = cell_ref[t : t + 1, :]
            at_row = jnp.broadcast_to(cell // LANES, (8, LANES))
            at_lane = jnp.broadcast_to(cell % LANES, (8, LANES))
            halves = []
            for half in range(0, BLOCK, 8):
                taken = jnp.zeros((8, LANES), f32)
                for y in range(ROWS):
                    values = source[
                        y + FSTEPS, half : half + 8, t * LANES : (t + 1) * LANES
                    ]
                    picked = jnp.take_along_axis(
                        values, at_lane, axis=1, mode="promise_in_bounds"
                    )
                    taken = jnp.where(at_row == y, picked, taken)
                halves.append(taken)
            at = pl.multiple_of(before + start, BLOCK)
            sample_ref[pl.ds(at, BLOCK), t * LANES : (t + 1) * LANES] = jnp.concatenate(
                halves, axis=0
            ).astype(bf16)
        for y in range(ROWS):
            field_ref[y, pl.ds(start, BLOCK), :] = source[y + FSTEPS].astype(bf16)
        return carry

    lax.fori_loop(0, m // BLOCK, block, 0)


def forecast(first, m, place, own, beside, cell, extra):
    width = own[0].shape[1]
    total = ROWS + 2 * FSTEPS
    outs = []
    if first:
        outs.append(jax.ShapeDtypeStruct((3, total, width), f32))
    rows = m + (BLOCK if first else extra[1].shape[0])
    outs.append(jax.ShapeDtypeStruct((rows, width), bf16))
    outs.append(jax.ShapeDtypeStruct((ROWS, m, width), bf16))
    args = (place,) + tuple(own) + tuple(beside) + (cell,) + tuple(extra)
    scratch = [pltpu.VMEM((total, BLOCK, width), f32)] * 2
    specs = [smem()] + [vmem()] * 5 + ([vmem()] * 2 + [smem()] * 2 if first else [vmem()] * 2)
    return call(
        functools.partial(forecast_kernel, first, m),
        outs,
        scratch,
        140 * 10**6 * m,
        args,
        specs,
    )


def reach_kernel(groups, place_ref, near_ref, own_ref, far_ref, *rest):
    parts, padded = rest[:-1], rest[-1]
    rows, width = own_ref.shape
    span = 2 * width // groups
    me, is_odd = place_ref[0], place_ref[1]
    facts = rows - BLOCK
    own = own_ref[facts:, :].astype(f32)
    for i, ref in ((1 - is_odd, near_ref), (is_odd, far_ref)):
        padded[i, :, :LANES] = jnp.zeros((rows, LANES), bf16)
        padded[i, :, LANES + width :] = jnp.zeros((rows, LANES), bf16)
        padded[i, :facts, LANES : LANES + width] = ref[:facts, :]
        padded[i, facts:, LANES : LANES + width] = jnp.concatenate(
            [ref[facts:, :].astype(f32)[:8], own[:8]], axis=0
        ).astype(bf16)
    for k, part in enumerate(parts):
        column = pl.multiple_of((me // 2 ^ k) * span, LANES)
        for i in range(2):
            part[i] = padded[i, :, pl.ds(column, span + 2 * LANES)]


def reached(groups, place, near, own, far):
    rows, width = own.shape
    wide = 2 * width // groups + 2 * LANES
    return call(
        functools.partial(reach_kernel, groups),
        [jax.ShapeDtypeStruct((2, rows, wide), bf16) for _ in range(groups // 2)],
        [pltpu.VMEM((2, rows, width + 2 * LANES), bf16)],
        0,
        (place, near, own, far),
        [smem()] + [vmem()] * 3,
    )


def merge_kernel(half, chunks, patches, place_ref, cell_ref, *rest):
    sample_refs = rest[:half]
    field_refs = rest[half : half + half * len(chunks)]
    mine, theirs, taken = rest[half + half * len(chunks) :]
    core = place_ref[0] % 2
    first = (place_ref[0] - core) * patches - 1
    strip = cell_ref.shape[0]
    tile_trials = sum(chunks)
    span = patches * LANES
    wide = span + 2 * LANES
    for t in range(2 * patches + 2):
        patch = jnp.clip(first + t, 0, strip - 1)
        cell = cell_ref[pl.ds(patch, 1), :]
        at_row = jnp.broadcast_to(cell // LANES, (8, LANES))
        at_lane = jnp.broadcast_to(cell % LANES, (8, LANES))
        column = pl.multiple_of(patch * LANES, LANES)
        at = 0
        for ref in field_refs:
            for k in range(0, ref.shape[1], BLOCK):
                picked = [jnp.zeros((8, LANES), f32), jnp.zeros((8, LANES), f32)]
                for y in range(ROWS):
                    entry = ref[y, k : k + BLOCK, pl.ds(column, LANES)].astype(f32)
                    here = at_row == y
                    for h in range(2):
                        values = jnp.take_along_axis(
                            entry[8 * h : 8 * h + 8],
                            at_lane,
                            axis=1,
                            mode="promise_in_bounds",
                        )
                        picked[h] = jnp.where(here, values, picked[h])
                taken[at : at + BLOCK, t * LANES : (t + 1) * LANES] = jnp.concatenate(
                    picked, axis=0
                ).astype(bf16)
                at += BLOCK
    for ref, column in ((mine, core * span), (theirs, (1 - core) * span)):
        cut = pl.ds(pl.multiple_of(column, LANES), wide)
        for k in range(half):
            at = 3 * k * tile_trials
            ref[at : at + tile_trials, :] = sample_refs[k][0, :tile_trials, cut]
            at += tile_trials
            ref[at : at + tile_trials, :] = taken[k * tile_trials : (k + 1) * tile_trials, cut]
            at += tile_trials
            ref[at : at + tile_trials, :] = sample_refs[k][1, :tile_trials, cut]
        for i in range(2):
            facts = sum(x[i, tile_trials:, cut].astype(f32) for x in sample_refs)
            at = 3 * half * tile_trials + i * BLOCK
            ref[at : at + BLOCK, :] = facts.astype(bf16)


def merged(chunks, patches, place, cell, samples, fields):
    half = len(samples)
    args = (place, cell) + tuple(samples) + tuple(fields)
    tile_trials = sum(chunks)
    shape = (3 * half * tile_trials + 2 * BLOCK, (patches + 2) * LANES)
    return call(
        functools.partial(merge_kernel, half, chunks, patches),
        [jax.ShapeDtypeStruct(shape, bf16)] * 2,
        [pltpu.VMEM((half * tile_trials, (2 * patches + 2) * LANES), bf16)],
        10**9,
        args,
        [smem()] + [vmem()] * (len(args) - 1),
    )


def product(a, b):
    return jnp.dot(a, b, preferred_element_type=f32)


def halves_of(a):
    high = a.astype(bf16)
    return high, (a - high.astype(f32)).astype(bf16)


def wide_product(a, b):
    return product(a[0], b[0]) + (product(a[0], b[1]) + product(a[1], b[0]))


def transform_kernel(groups, even_ref, odd_ref, *rest):
    outs = rest[:groups]
    values = rest[groups]
    _, members, width = values.shape
    wide = width // LANES
    patches = wide - 2
    tile_trials = members // groups
    for d in range(groups):
        ref = odd_ref if d % 2 else even_ref
        at = d * tile_trials
        for i in range(3):
            start = (3 * (d // 2) + i) * tile_trials
            values[i, at : at + tile_trials, :] = ref[start : start + tile_trials, :]
    last = 3 * (groups // 2) * tile_trials
    both = even_ref[last:, :].astype(f32) + odd_ref[last:, :].astype(f32)
    facts = (both[:BLOCK], both[BLOCK:])
    about = []
    for terms in (facts[0][:8], facts[0][8:], facts[1][:8]):
        about.append(
            (
                (terms[0:1] + terms[1:2]) + terms[2:3],
                (terms[3:4] + terms[4:5]) + terms[5:6],
                terms[6:7],
                terms[7:8],
            )
        )
    deviation = [[None] * wide for _ in range(3)]
    gap = [[None] * wide for _ in range(3)]
    for i in range(3):
        for t in range(wide):
            cut = slice(t * LANES, (t + 1) * LANES)
            entry = values[i, :, cut].astype(f32)
            average = jnp.sum(entry, axis=0, keepdims=True) * (1.0 / members)
            deviation[i][t] = entry - average
            gap[i][t] = about[i][0][:, cut] - average
    factor = float(members - 1)
    row_id = lax.broadcasted_iota(jnp.int32, (members, members), 0)
    col_id = lax.broadcasted_iota(jnp.int32, (members, members), 1)
    diagonal = row_id == col_id
    state = []
    for q in range(patches):
        pieces = []
        pull = jnp.zeros((members, LANES), f32)
        for i in range(3):
            for t in range(q, q + 3):
                cut = slice(t * LANES, (t + 1) * LANES)
                inverse = about[i][1][:, cut]
                cell_y = about[i][2][:, cut]
                cell_x = about[i][3][:, cut]
                off_y = ((i - 1) * ROWS + cell_y - (ROWS - 1) / 2.0) / ROWS
                off_x = ((t - q - 1) * LANES + cell_x - (LANES - 1) / 2.0) / LANES
                local = inverse * jnp.exp(-0.5 * off_y * off_y - 0.5 * off_x * off_x)
                weight = jnp.sqrt(local * (1.0 / factor))
                pieces.append((deviation[i][t] * weight).astype(bf16))
                pull = pull + deviation[i][t] * (local * (1.0 / factor) * gap[i][t])
        scaled = jnp.concatenate(pieces, axis=1)
        gram = lax.dot_general(
            scaled, scaled, (((1,), (1,)), ((), ())), preferred_element_type=f32
        )
        system = jnp.where(diagonal, gram + 1.0, gram)
        squared = jnp.sum(system * system, axis=0, keepdims=True)
        squared = jnp.sum(squared, axis=1, keepdims=True)
        scale = jnp.sqrt(squared)
        state.append([system * (1.0 / scale), None, scale, jnp.sum(pull, axis=1, keepdims=True)])
    for step in range(NSIT):
        fine = step >= NSIT - 2
        for s in state:
            w, z = s[0], s[1]
            if fine:
                half = halves_of(w * -0.5)
                mul = lambda a: wide_product(halves_of(a), half)
            else:
                half = (w * -0.5).astype(bf16)
                mul = lambda a: product(a.astype(bf16), half)
            if z is None:
                s[1] = jnp.where(diagonal, 1.5, 0.0) - 0.5 * w
            else:
                s[1] = 1.5 * z + mul(z)
            if step < NSIT - 1:
                between = 1.5 * w + mul(w)
                s[0] = 1.5 * between + mul(between)
    for q in range(patches):
        _, z, scale, pull = state[q]
        root = z * lax.rsqrt(scale)
        pull = jnp.sum(jnp.where(diagonal, pull, 0.0), axis=0, keepdims=True)
        once = jnp.sum(root * pull, axis=1, keepdims=True)
        gain = jnp.sum(root * once, axis=0, keepdims=True)
        middle = jnp.sum(root, axis=1, keepdims=True) * (1.0 / members)
        shift = gain - jnp.sum(gain, axis=1, keepdims=True) * (1.0 / members) + 1.0 / members
        mixing = ((root - middle) + shift).astype(bf16)
        for d in range(groups):
            outs[d][q] = mixing[d * tile_trials : (d + 1) * tile_trials, :]


def transform(groups, tile_trials, even, odd):
    wide = even.shape[1]
    members = groups * tile_trials
    return call(
        functools.partial(transform_kernel, groups),
        [
            jax.ShapeDtypeStruct((wide // LANES - 2, tile_trials, members), bf16)
            for _ in range(groups)
        ],
        [pltpu.VMEM((3, members, wide), bf16)],
        4 * 10**9,
        (even, odd),
        [vmem()] * 2,
    )


def analysis_kernel(groups, chunks, place_ref, *rest):
    mixing_refs = rest[:groups]
    count = groups * len(chunks)
    field_refs = rest[groups : groups + count]
    out_ref, turned = rest[groups + count :]
    patches, tile_trials, _ = mixing_refs[0].shape
    me = place_ref[0]
    for e in range(groups):
        for q in range(patches):
            column = pl.multiple_of(((me ^ e) * patches + q) * LANES, LANES)
            pieces = []
            for y in range(ROWS):
                stack = [
                    field_refs[j * groups + (k ^ e)][y, :, pl.ds(column, LANES)]
                    for k in range(groups)
                    for j in range(len(chunks))
                ]
                pieces.append(jnp.concatenate(stack, axis=0))
            result = product(mixing_refs[e][q], jnp.concatenate(pieces, axis=1))
            for y in range(ROWS):
                turned[pl.ds(y, tile_trials, stride=ROWS), :] = result[
                    :, y * LANES : (y + 1) * LANES
                ]
            out_ref[:, :, pl.ds(column, LANES)] = (
                turned[...].reshape(tile_trials, ROWS, LANES).astype(bf16)
            )


def analysed(groups, chunks, place, mixing, fields):
    tile_trials = sum(chunks)
    width = fields[0].shape[2]
    args = (place,) + tuple(mixing) + tuple(fields)
    return call(
        functools.partial(analysis_kernel, groups, chunks),
        [jax.ShapeDtypeStruct((tile_trials, ROWS, width), bf16)],
        [pltpu.VMEM((tile_trials * ROWS, LANES), f32)],
        2 * tile_trials * tile_trials * groups * ROWS * width,
        args,
        [smem()] + [vmem()] * (len(args) - 1),
    )[0]


def across(parts):
    groups = len(parts)
    out = list(parts)
    for d in sorted(range(1, groups), reverse=True):
        out[d] = lax.ppermute(parts[d], "cols", [(i, i ^ d) for i in range(groups)])
    return out


def everywhere(held, bits, groups):
    held = dict(held)
    for bit in bits:
        pairs = [(i, i ^ bit) for i in range(groups)]
        held.update({d ^ bit: lax.ppermute(x, "cols", pairs) for d, x in held.items()})
    return held


def after(x, other):
    return lax.optimization_barrier((x, other))[0]


def beside(to_near, to_far):
    count = lax.axis_size("rows")
    near = [(i, i ^ 1) for i in range(count) if i ^ 1 < count]
    far = [(i, i + 1) for i in range(1, count - 1, 2)]
    far += [(j, i) for i, j in far]
    return lax.ppermute(to_near, "rows", near), lax.ppermute(to_far, "rows", far)


def on_device(
    prior_trials, courant, diffusion, obs_cell, obs_count, obs_value, error_kind, error_std
):
    tile_trials = prior_trials.shape[0]
    groups = lax.axis_size("cols")
    place = jnp.stack([lax.axis_index("cols"), lax.axis_index("rows") % 2]).astype(jnp.int32)
    half = tile_trials // 2
    chunks = (half, half) if half % BLOCK == 0 else (tile_trials,)

    bits = [1 << k for k in reversed(range(groups.bit_length() - 1))]

    messages = packed(chunks, place, prior_trials, courant, diffusion)
    halos = []
    for j in range(len(chunks)):
        pair = messages[2 * j : 2 * j + 2]
        if j:
            pair, halos[j - 1] = lax.optimization_barrier((pair, halos[j - 1]))
        halos.append(beside(*pair))
    coef, sampled, fields = None, None, []
    for j, m in enumerate(chunks):
        extra = (obs_value, error_kind, obs_count, error_std) if j == 0 else (coef, sampled)
        made = forecast(
            j == 0, m, place, messages[2 * j : 2 * j + 2], halos[j], obs_cell[0], extra
        )
        if j == 0:
            coef, made = made[0], made[1:]
        sampled, field = made
        fields.append(everywhere({0: field}, bits[:-1], groups))
    near, far = beside(sampled, sampled)
    samples = list(reached(groups, place, near, sampled, far))
    for k in range(1, groups // 2):
        samples[k] = lax.ppermute(samples[k], "cols", [(i, i ^ 2 * k) for i in range(groups)])
    held = [field[d] for d in range(0, groups, 2) for field in fields]
    mine, theirs = merged(chunks, obs_count.shape[1], place, obs_cell[0], samples, held)
    theirs = lax.ppermute(theirs, "cols", [(i, i ^ 1) for i in range(groups)])
    mixing = transform(groups, tile_trials, mine, theirs)
    fields = [everywhere(after(field, mine), bits[-1:], groups) for field in fields]
    fields = [field[d] for field in fields for d in range(groups)]
    return analysed(groups, chunks, place, across(after(mixing, fields)), fields)


def solution(mesh):
    placed = (
        P("cols", "rows", None),
        P("rows", None),
        P("rows", None),
        P("rows", None, None),
        P("rows", "cols"),
        P("rows", "cols", None),
        P("rows", "cols", None),
        P(),
    )
    return jax.shard_map(
        on_device, mesh=mesh, in_specs=placed, out_specs=P("cols", "rows", None), check_vma=False
    )
```

```python
import functools
import math
import jax
import jax.numpy as jnp
from jax import lax
from jax.experimental import pallas as pl
from jax.experimental.pallas import tpu as pltpu
from jax.sharding import PartitionSpec as P

ROWS = 8
LANES = 128
FSTEPS = 4
NSIT = 6
BLOCK = 16
SLACK = 12 * 1024 * 1024
f32 = jnp.float32
bf16 = jnp.bfloat16

vmem = functools.partial(pl.BlockSpec, memory_space=pltpu.VMEM)
smem = functools.partial(pl.BlockSpec, memory_space=pltpu.SMEM)


def call(kernel, outs, scratch, flops, args, specs):
    moved = sum(x.size * x.dtype.itemsize for x in tuple(args) + tuple(outs))
    held = sum(math.prod(x.shape) * jnp.dtype(x.dtype).itemsize for x in scratch)
    return pl.pallas_call(
        kernel,
        out_shape=outs,
        in_specs=specs,
        out_specs=[vmem() for _ in outs],
        scratch_shapes=scratch,
        compiler_params=pltpu.CompilerParams(vmem_limit_bytes=moved + held + SLACK),
        cost_estimate=pl.CostEstimate(flops=flops, bytes_accessed=moved, transcendentals=0),
    )(*args)


def pack_kernel(offset, m, me_ref, odd_ref, prior_ref, *rest):
    flat = rest[-1]
    if offset == 0:
        speed_ref, spread_ref, cell_ref = rest[:3]
        pair, cells_ref = rest[3:5], rest[5]
        cells_ref[...] = cell_ref[...]
    else:
        pair = rest[:2]
    odd = odd_ref[0]

    def fill(first_low, second_low):
        def block(i, carry):
            start = pl.multiple_of(i * BLOCK, BLOCK)
            for t in range(flat.shape[0]):
                cut = slice(t * LANES, (t + 1) * LANES)
                entry = prior_ref[pl.ds(offset + start, BLOCK), :, cut].astype(f32)
                flat[t] = entry.reshape(BLOCK * ROWS, LANES)
                for ref, low in zip(pair, (first_low, second_low)):
                    for r in range(FSTEPS):
                        at = pl.multiple_of(r * m + start, BLOCK)
                        ref[pl.ds(at, BLOCK), cut] = flat[
                            t, pl.ds(low + r, BLOCK, stride=ROWS), :
                        ].astype(bf16)
            return carry

        lax.fori_loop(0, m // BLOCK, block, 0)
        if offset == 0:
            speed = speed_ref[...].astype(f32)
            spread = spread_ref[...].astype(f32)
            blank = jnp.zeros((BLOCK - 2 * FSTEPS, speed.shape[1]), f32)
            for ref, low in zip(pair, (first_low, second_low)):
                ref[FSTEPS * m :, :] = jnp.concatenate(
                    [speed[low : low + FSTEPS], spread[low : low + FSTEPS], blank], axis=0
                ).astype(bf16)

    pl.when(odd == 1)(lambda: fill(0, FSTEPS))
    pl.when(odd == 0)(lambda: fill(FSTEPS, 0))


def packed(offset, m, place, prior, extra):
    width = prior.shape[2]
    rows = FSTEPS * m + (BLOCK if offset == 0 else 0)
    outs = [jax.ShapeDtypeStruct((rows, width), bf16)] * 2
    if offset == 0:
        outs.append(jax.ShapeDtypeStruct(extra[2].shape, extra[2].dtype))
    args = place + (prior,) + tuple(extra)
    return call(
        functools.partial(pack_kernel, offset, m),
        outs,
        [pltpu.VMEM((width // LANES, BLOCK * ROWS, LANES), f32)],
        0,
        args,
        [smem()] * 2 + [vmem()] * (len(args) - 2),
    )


def thirds_of(x):
    high = x.astype(bf16).astype(f32)
    middle = (x - high).astype(bf16).astype(f32)
    return [high, middle, (x - high) - middle]


def describe(m, me, sample_ref, cell_ref, value_ref, kind_ref, count_ref, std_ref):
    sample_ref[m : m + BLOCK, :] = jnp.zeros((BLOCK, sample_ref.shape[1]), bf16)
    own_count, slots = value_ref.shape[1:]
    slot = lax.broadcasted_iota(jnp.int32, (1, slots), 1)
    blank = jnp.zeros((BLOCK - 8, slots), f32)
    for q in range(own_count):
        patch = me * own_count + q
        cell = cell_ref[pl.ds(patch, 1), :]
        kind = kind_ref[0, q : q + 1, :]
        inverse = jnp.zeros((1, slots), f32)
        for k in range(std_ref.shape[0]):
            deviation = jnp.full((1, slots), std_ref[k], f32)
            inverse = jnp.where(kind == k, 1.0 / (deviation * deviation), inverse)
        inverse = jnp.where(slot < count_ref[0, q], inverse, 0.0)
        terms = thirds_of(value_ref[0, q : q + 1, :]) + thirds_of(inverse)
        terms += [(cell // LANES).astype(f32), (cell % LANES).astype(f32), blank]
        column = pl.multiple_of(patch * LANES, LANES)
        sample_ref[m : m + BLOCK, pl.ds(column, LANES)] = jnp.concatenate(
            terms, axis=0
        ).astype(bf16)


def forecast_kernel(
    first, m, me_ref, odd_ref, near_ref, far_ref, from_near_ref, from_far_ref, cell_ref, *rest
):
    if first:
        value_ref, kind_ref, count_ref, std_ref, coef_ref, sample_ref = rest[:6]
        rest = rest[6:]
        before = 0
    else:
        coef_ref, earlier_ref, sample_ref = rest[:3]
        rest = rest[3:]
        before = earlier_ref.shape[0] - BLOCK
        sample_ref[:before, :] = earlier_ref[:before, :]
        sample_ref[before + m :, :] = earlier_ref[before:, :]
    field_ref, even, odd = rest
    width = near_ref.shape[1]
    tiles = width // LANES
    total = ROWS + 2 * FSTEPS
    me, is_odd = me_ref[0], odd_ref[0]
    sources = (
        (from_near_ref, (1 - is_odd) * (FSTEPS + ROWS)),
        (near_ref, FSTEPS + (1 - is_odd) * FSTEPS),
        (far_ref, FSTEPS + is_odd * FSTEPS),
        (from_far_ref, is_odd * (FSTEPS + ROWS)),
    )
    if first:
        base = FSTEPS * m
        tails = [ref[base : base + BLOCK, :].astype(f32) for ref, _ in sources]
        tails = [jnp.where(is_odd == 1, tails[k], tails[3 - k]) for k in range(4)]
        speed = jnp.concatenate([x[:FSTEPS] for x in tails], axis=0)
        spread = jnp.concatenate([x[FSTEPS : 2 * FSTEPS] for x in tails], axis=0)
        coef_ref[0] = 1.0 - speed - 4.0 * spread
        coef_ref[1] = speed + spread
        coef_ref[2] = spread
        describe(m, me, sample_ref, cell_ref, value_ref, kind_ref, count_ref, std_ref)
    lane = lax.broadcasted_iota(jnp.int32, (8, LANES), 1)
    leftmost = lane == 0
    rightmost = lane == LANES - 1

    def block(i, carry):
        start = pl.multiple_of(i * BLOCK, BLOCK)
        for ref, first_row in sources:
            for r in range(FSTEPS):
                at = pl.multiple_of(r * m + start, BLOCK)
                even[first_row + r] = ref[pl.ds(at, BLOCK), :].astype(f32)
        source, target = even, odd
        for step in range(1, FSTEPS + 1):
            for half in range(0, BLOCK, 8):

                def row(r):
                    return [
                        source[r, half : half + 8, t * LANES : (t + 1) * LANES]
                        for t in range(tiles)
                    ]

                above, centre = row(step - 1), row(step)
                for r in range(step, total - step):
                    below = row(r + 1)
                    right = [pltpu.roll(c, 1, 1) for c in centre]
                    left = [pltpu.roll(c, LANES - 1, 1) for c in centre]
                    for t in range(tiles):
                        cut = slice(t * LANES, (t + 1) * LANES)
                        west = jnp.where(leftmost, right[t - 1] if t else 0.0, right[t])
                        east = jnp.where(
                            rightmost, left[t + 1] if t + 1 < tiles else 0.0, left[t]
                        )
                        target[r, half : half + 8, cut] = (
                            coef_ref[0, r : r + 1, cut] * centre[t]
                            + coef_ref[1, r : r + 1, cut] * above[t]
                            + coef_ref[2, r : r + 1, cut] * (below[t] + (west + east))
                        )
                    above, centre = centre, below
            source, target = target, source
        for t in range(tiles):
            cell = cell_ref[t : t + 1, :]
            at_row = jnp.broadcast_to(cell // LANES, (8, LANES))
            at_lane = jnp.broadcast_to(cell % LANES, (8, LANES))
            halves = []
            for half in range(0, BLOCK, 8):
                taken = jnp.zeros((8, LANES), f32)
                for y in range(ROWS):
                    values = source[
                        y + FSTEPS, half : half + 8, t * LANES : (t + 1) * LANES
                    ]
                    picked = jnp.take_along_axis(
                        values, at_lane, axis=1, mode="promise_in_bounds"
                    )
                    taken = jnp.where(at_row == y, picked, taken)
                halves.append(taken)
            at = pl.multiple_of(before + start, BLOCK)
            sample_ref[pl.ds(at, BLOCK), t * LANES : (t + 1) * LANES] = jnp.concatenate(
                halves, axis=0
            ).astype(bf16)
        for y in range(ROWS):
            field_ref[y, pl.ds(start, BLOCK), :] = source[y + FSTEPS].astype(bf16)
        return carry

    lax.fori_loop(0, m // BLOCK, block, 0)


def forecast(first, m, place, own, beside, cell, extra):
    width = own[0].shape[1]
    total = ROWS + 2 * FSTEPS
    outs = []
    if first:
        outs.append(jax.ShapeDtypeStruct((3, total, width), f32))
    rows = m + (BLOCK if first else extra[1].shape[0])
    outs.append(jax.ShapeDtypeStruct((rows, width), bf16))
    outs.append(jax.ShapeDtypeStruct((ROWS, m, width), bf16))
    args = place + tuple(own) + tuple(beside) + (cell,) + tuple(extra)
    scratch = [pltpu.VMEM((total, BLOCK, width), f32)] * 2
    specs = [smem()] * 2 + [vmem()] * 5 + ([vmem()] * 2 + [smem()] * 2 if first else [vmem()] * 2)
    return call(
        functools.partial(forecast_kernel, first, m),
        outs,
        scratch,
        140 * 10**6 * m,
        args,
        specs,
    )


def reach_kernel(groups, me_ref, odd_ref, near_ref, own_ref, far_ref, *rest):
    parts, padded = rest[:-1], rest[-1]
    rows, width = own_ref.shape
    span = 2 * width // groups
    me, is_odd = me_ref[0], odd_ref[0]
    facts = rows - BLOCK
    own = own_ref[facts:, :].astype(f32)
    for i, ref in ((1 - is_odd, near_ref), (is_odd, far_ref)):
        padded[i, :, :LANES] = jnp.zeros((rows, LANES), bf16)
        padded[i, :, LANES + width :] = jnp.zeros((rows, LANES), bf16)
        padded[i, :facts, LANES : LANES + width] = ref[:facts, :]
        padded[i, facts:, LANES : LANES + width] = jnp.concatenate(
            [ref[facts:, :].astype(f32)[:8], own[:8]], axis=0
        ).astype(bf16)
    for k, part in enumerate(parts):
        column = pl.multiple_of((me // 2 ^ k) * span, LANES)
        for i in range(2):
            part[i] = padded[i, :, pl.ds(column, span + 2 * LANES)]


def reached(groups, place, near, own, far):
    rows, width = own.shape
    wide = 2 * width // groups + 2 * LANES
    return call(
        functools.partial(reach_kernel, groups),
        [jax.ShapeDtypeStruct((2, rows, wide), bf16) for _ in range(groups // 2)],
        [pltpu.VMEM((2, rows, width + 2 * LANES), bf16)],
        0,
        place + (near, own, far),
        [smem()] * 2 + [vmem()] * 3,
    )


def take_kernel(patches, me_ref, odd_ref, cell_ref, *rest):
    field_refs, taken = rest[:-1], rest[-1]
    first = me_ref[0] // 2 * 2 * patches - 1
    strip = cell_ref.shape[0]
    for t in range(2 * patches + 2):
        patch = jnp.clip(first + t, 0, strip - 1)
        cell = cell_ref[pl.ds(patch, 1), :]
        at_row = jnp.broadcast_to(cell // LANES, (8, LANES))
        at_lane = jnp.broadcast_to(cell % LANES, (8, LANES))
        column = pl.multiple_of(patch * LANES, LANES)
        at = 0
        for ref in field_refs:
            for k in range(0, ref.shape[1], BLOCK):
                picked = [jnp.zeros((8, LANES), f32), jnp.zeros((8, LANES), f32)]
                for y in range(ROWS):
                    entry = ref[y, k : k + BLOCK, pl.ds(column, LANES)].astype(f32)
                    here = at_row == y
                    for h in range(2):
                        values = jnp.take_along_axis(
                            entry[8 * h : 8 * h + 8],
                            at_lane,
                            axis=1,
                            mode="promise_in_bounds",
                        )
                        picked[h] = jnp.where(here, values, picked[h])
                taken[at : at + BLOCK, t * LANES : (t + 1) * LANES] = jnp.concatenate(
                    picked, axis=0
                ).astype(bf16)
                at += BLOCK


def taken_here(patches, place, cell, fields):
    members = sum(x.shape[1] for x in fields)
    args = place + (cell,) + tuple(fields)
    return call(
        functools.partial(take_kernel, patches),
        [jax.ShapeDtypeStruct((members, (2 * patches + 2) * LANES), bf16)],
        [],
        10**9,
        args,
        [smem()] * 2 + [vmem()] * (len(args) - 2),
    )[0]


def merge_kernel(half, me_ref, odd_ref, taken, *rest):
    sample_refs = rest[:half]
    mine, theirs = rest[half:]
    core = me_ref[0] % 2
    tile_trials = taken.shape[0] // half
    wide = mine.shape[1]
    span = wide - 2 * LANES
    for ref, column in ((mine, core * span), (theirs, (1 - core) * span)):
        cut = pl.ds(pl.multiple_of(column, LANES), wide)
        for k in range(half):
            at = 3 * k * tile_trials
            ref[at : at + tile_trials, :] = sample_refs[k][0, :tile_trials, cut]
            at += tile_trials
            ref[at : at + tile_trials, :] = taken[k * tile_trials : (k + 1) * tile_trials, cut]
            at += tile_trials
            ref[at : at + tile_trials, :] = sample_refs[k][1, :tile_trials, cut]
        for i in range(2):
            facts = sum(x[i, tile_trials:, cut].astype(f32) for x in sample_refs)
            at = 3 * half * tile_trials + i * BLOCK
            ref[at : at + BLOCK, :] = facts.astype(bf16)


def merged(place, taken, samples):
    half = len(samples)
    shape = (3 * taken.shape[0] + 2 * BLOCK, taken.shape[1] // 2 + LANES)
    args = place + (taken,) + tuple(samples)
    return call(
        functools.partial(merge_kernel, half),
        [jax.ShapeDtypeStruct(shape, bf16)] * 2,
        [],
        0,
        args,
        [smem()] * 2 + [vmem()] * (len(args) - 2),
    )


def product(a, b):
    return jnp.dot(a, b, preferred_element_type=f32)


def halves_of(a):
    high = a.astype(bf16)
    return high, (a - high.astype(f32)).astype(bf16)


def wide_product(a, b):
    return product(a[0], b[0]) + (product(a[0], b[1]) + product(a[1], b[0]))


def transform_kernel(groups, even_ref, odd_ref, *rest):
    outs = rest[:groups]
    values = rest[groups]
    _, members, width = values.shape
    wide = width // LANES
    patches = wide - 2
    tile_trials = members // groups
    for d in range(groups):
        ref = odd_ref if d % 2 else even_ref
        at = d * tile_trials
        for i in range(3):
            start = (3 * (d // 2) + i) * tile_trials
            values[i, at : at + tile_trials, :] = ref[start : start + tile_trials, :]
    last = 3 * (groups // 2) * tile_trials
    both = even_ref[last:, :].astype(f32) + odd_ref[last:, :].astype(f32)
    facts = (both[:BLOCK], both[BLOCK:])
    about = []
    for terms in (facts[0][:8], facts[0][8:], facts[1][:8]):
        about.append(
            (
                (terms[0:1] + terms[1:2]) + terms[2:3],
                (terms[3:4] + terms[4:5]) + terms[5:6],
                terms[6:7],
                terms[7:8],
            )
        )
    deviation = [[None] * wide for _ in range(3)]
    gap = [[None] * wide for _ in range(3)]
    for i in range(3):
        for t in range(wide):
            cut = slice(t * LANES, (t + 1) * LANES)
            entry = values[i, :, cut].astype(f32)
            average = jnp.sum(entry, axis=0, keepdims=True) * (1.0 / members)
            deviation[i][t] = entry - average
            gap[i][t] = about[i][0][:, cut] - average
    factor = float(members - 1)
    row_id = lax.broadcasted_iota(jnp.int32, (members, members), 0)
    col_id = lax.broadcasted_iota(jnp.int32, (members, members), 1)
    diagonal = row_id == col_id
    state = []
    for q in range(patches):
        pieces = []
        pull = jnp.zeros((members, LANES), f32)
        for i in range(3):
            for t in range(q, q + 3):
                cut = slice(t * LANES, (t + 1) * LANES)
                inverse = about[i][1][:, cut]
                cell_y = about[i][2][:, cut]
                cell_x = about[i][3][:, cut]
                off_y = ((i - 1) * ROWS + cell_y - (ROWS - 1) / 2.0) / ROWS
                off_x = ((t - q - 1) * LANES + cell_x - (LANES - 1) / 2.0) / LANES
                local = inverse * jnp.exp(-0.5 * off_y * off_y - 0.5 * off_x * off_x)
                weight = jnp.sqrt(local * (1.0 / factor))
                pieces.append((deviation[i][t] * weight).astype(bf16))
                pull = pull + deviation[i][t] * (local * (1.0 / factor) * gap[i][t])
        scaled = jnp.concatenate(pieces, axis=1)
        gram = lax.dot_general(
            scaled, scaled, (((1,), (1,)), ((), ())), preferred_element_type=f32
        )
        system = jnp.where(diagonal, gram + 1.0, gram)
        squared = jnp.sum(system * system, axis=0, keepdims=True)
        squared = jnp.sum(squared, axis=1, keepdims=True)
        scale = jnp.sqrt(squared)
        state.append([system * (1.0 / scale), None, scale, jnp.sum(pull, axis=1, keepdims=True)])
    for step in range(NSIT):
        fine = step >= NSIT - 2
        for s in state:
            w, z = s[0], s[1]
            if fine:
                half = halves_of(w * -0.5)
                mul = lambda a: wide_product(halves_of(a), half)
            else:
                half = (w * -0.5).astype(bf16)
                mul = lambda a: product(a.astype(bf16), half)
            if z is None:
                s[1] = jnp.where(diagonal, 1.5, 0.0) - 0.5 * w
            else:
                s[1] = 1.5 * z + mul(z)
            if step < NSIT - 1:
                between = 1.5 * w + mul(w)
                s[0] = 1.5 * between + mul(between)
    for q in range(patches):
        _, z, scale, pull = state[q]
        root = z * lax.rsqrt(scale)
        pull = jnp.sum(jnp.where(diagonal, pull, 0.0), axis=0, keepdims=True)
        once = jnp.sum(root * pull, axis=1, keepdims=True)
        gain = jnp.sum(root * once, axis=0, keepdims=True)
        middle = jnp.sum(root, axis=1, keepdims=True) * (1.0 / members)
        shift = gain - jnp.sum(gain, axis=1, keepdims=True) * (1.0 / members) + 1.0 / members
        mixing = ((root - middle) + shift).astype(bf16)
        for d in range(groups):
            outs[d][q] = mixing[d * tile_trials : (d + 1) * tile_trials, :]


def transform(groups, tile_trials, even, odd):
    wide = even.shape[1]
    members = groups * tile_trials
    return call(
        functools.partial(transform_kernel, groups),
        [
            jax.ShapeDtypeStruct((wide // LANES - 2, tile_trials, members), bf16)
            for _ in range(groups)
        ],
        [pltpu.VMEM((3, members, wide), bf16)],
        4 * 10**9,
        (even, odd),
        [vmem()] * 2,
    )


def analysis_kernel(groups, chunks, turns, me_ref, odd_ref, *rest):
    mixing_refs = rest[: len(turns)]
    count = groups * len(chunks)
    field_refs = rest[len(turns) : len(turns) + count]
    out_ref, ready, turned, sems = rest[-4:]
    patches, tile_trials, _ = mixing_refs[0].shape
    me = me_ref[0]
    copies = []
    for e, mixing_ref in zip(turns, mixing_refs):
        for q in range(patches):
            column = pl.multiple_of(((me ^ e) * patches + q) * LANES, LANES)
            pieces = []
            for y in range(ROWS):
                stack = [
                    field_refs[j * groups + (k ^ e)][y, :, pl.ds(column, LANES)]
                    for k in range(groups)
                    for j in range(len(chunks))
                ]
                pieces.append(jnp.concatenate(stack, axis=0))
            result = product(mixing_ref[q], jnp.concatenate(pieces, axis=1))
            at = len(copies)
            for y in range(ROWS):
                turned[at % 2, pl.ds(y, tile_trials, stride=ROWS), :] = result[
                    :, y * LANES : (y + 1) * LANES
                ]
            ready[at] = turned[at % 2].reshape(tile_trials, ROWS, LANES).astype(bf16)
            copy = pltpu.make_async_copy(
                ready.at[at], out_ref.at[:, :, pl.ds(column, LANES)], sems.at[at]
            )
            copy.start()
            copies.append(copy)
    for copy in copies:
        copy.wait()


def analysed(groups, chunks, turns, place, mixing, fields, begun):
    patches, tile_trials, _ = mixing[0].shape
    width = fields[0].shape[2]
    args = place + tuple(mixing[e] for e in turns) + tuple(fields)
    specs = [smem()] * 2 + [vmem()] * (len(args) - 2)
    aliases = {}
    if begun is not None:
        aliases = {len(args): 0}
        args += (begun,)
        specs.append(pl.BlockSpec(memory_space=pl.ANY))
    out = jax.ShapeDtypeStruct((tile_trials, ROWS, width), bf16)
    count = len(turns) * patches
    moved = sum(x.size * x.dtype.itemsize for x in args) + 3 * out.size * 2
    return pl.pallas_call(
        functools.partial(analysis_kernel, groups, chunks, turns),
        out_shape=out,
        in_specs=specs,
        out_specs=pl.BlockSpec(memory_space=pl.ANY),
        scratch_shapes=[
            pltpu.VMEM((count, tile_trials, ROWS, LANES), bf16),
            pltpu.VMEM((2, tile_trials * ROWS, LANES), f32),
            pltpu.SemaphoreType.DMA((count,)),
        ],
        input_output_aliases=aliases,
        compiler_params=pltpu.CompilerParams(vmem_limit_bytes=moved + SLACK),
        cost_estimate=pl.CostEstimate(flops=10**9, bytes_accessed=moved, transcendentals=0),
    )(*args)


def across(parts):
    groups = len(parts)
    out = list(parts)
    for d in sorted(range(1, groups), reverse=True):
        out[d] = lax.ppermute(parts[d], "cols", [(i, i ^ d) for i in range(groups)])
    return out


def everywhere(held, bits, groups):
    held = dict(held)
    for bit in bits:
        pairs = [(i, i ^ bit) for i in range(groups)]
        held.update({d ^ bit: lax.ppermute(x, "cols", pairs) for d, x in held.items()})
    return held


def after(x, other):
    return lax.optimization_barrier((x, other))[0]


def beside(to_near, to_far):
    count = lax.axis_size("rows")
    near = [(i, i ^ 1) for i in range(count) if i ^ 1 < count]
    far = [(i, i + 1) for i in range(1, count - 1, 2)]
    far += [(j, i) for i, j in far]
    return lax.ppermute(to_near, "rows", near), lax.ppermute(to_far, "rows", far)


def on_device(
    prior_trials, courant, diffusion, obs_cell, obs_count, obs_value, error_kind, error_std
):
    tile_trials = prior_trials.shape[0]
    groups = lax.axis_size("cols")
    place = (lax.axis_index("cols")[None], (lax.axis_index("rows") % 2)[None])
    half = tile_trials // 2
    chunks = (half, half) if half % BLOCK == 0 else (tile_trials,)

    bits = [1 << k for k in reversed(range(groups.bit_length() - 1))]

    messages, halos = [], []
    for j, m in enumerate(chunks):
        extra = () if j else (courant, diffusion, obs_cell[0])
        made = packed(sum(chunks[:j]), m, place, prior_trials, extra)
        if j == 0:
            made, cells = made[:2], made[2]
        else:
            made, halos[j - 1] = lax.optimization_barrier((made, halos[j - 1]))
        messages += made
        halos.append(beside(*made))
    coef, sampled, fields = None, None, []
    for j, m in enumerate(chunks):
        extra = (obs_value, error_kind, obs_count, error_std) if j == 0 else (coef, sampled)
        made = forecast(
            j == 0, m, place, messages[2 * j : 2 * j + 2], halos[j], cells, extra
        )
        if j == 0:
            coef, made = made[0], made[1:]
        sampled, field = made
        fields.append(everywhere({0: field}, bits[:-1], groups))
    near, far = beside(sampled, sampled)
    samples = list(reached(groups, place, near, sampled, far))
    for k in range(1, groups // 2):
        samples[k] = lax.ppermute(samples[k], "cols", [(i, i ^ 2 * k) for i in range(groups)])
    held = [field[d] for d in range(0, groups, 2) for field in fields]
    taken = taken_here(obs_count.shape[1], place, cells, held)
    mine, theirs = merged(place, taken, samples)
    theirs = lax.ppermute(theirs, "cols", [(i, i ^ 1) for i in range(groups)])
    mixing = transform(groups, tile_trials, mine, theirs)
    fields = [everywhere(after(field, mine), bits[-1:], groups) for field in fields]
    fields = [field[d] for field in fields for d in range(groups)]
    mixing = across(after(mixing, fields))
    begun = analysed(groups, chunks, (0, 1), place, mixing, fields, None)
    return analysed(groups, chunks, tuple(range(2, groups)), place, mixing, fields, begun)


def solution(mesh):
    placed = (
        P("cols", "rows", None),
        P("rows", None),
        P("rows", None),
        P("rows", None, None),
        P("rows", "cols"),
        P("rows", "cols", None),
        P("rows", "cols", None),
        P(),
    )
    return jax.shard_map(
        on_device, mesh=mesh, in_specs=placed, out_specs=P("cols", "rows", None), check_vma=False
    )
```
